128 devices in a mesh: expert: 8 (over z, core), fsdp: 16 (over y, x).
Axes of the slice: x: 4, y: 4, z: 4, core: 2. Of those that a mesh axis runs over, the one named last changes fastest.
Arguments:
- gradient: bfloat16 [16, 7168, 2048], P('expert', 'fsdp'), may hold values from -6 to 6
- momentum: float32 [16, 7168, 2048], P('expert', 'fsdp'), may hold values from -6 to 6
- right_factor: float32 [16, 2048, 128], P('expert'), may hold values from -6 to 6
- placement: int32 [16], replicated, may hold values from 0 to 15, as said below
Outputs:
- new_momentum: float32 [16, 7168, 2048], P('expert', 'fsdp')
- new_right: float32 [16, 2048, 128], P('expert')
- left_at_owner: bfloat16 [16, 7168, 128], P('expert', 'fsdp')
- right_at_owner: bfloat16 [16, 2048, 128], P('expert', 'fsdp')
The draws below stay inside these ranges and needn't reach their ends.
Inputs may be any that keep to these rules, and one draw needn't show every extreme that they name: placement names each serving slot once; slot s belongs to index s // 2 of expert; expert 2i+j (j = 0, 1) is served on index (i+1) % 8 of expert if j = 0 and on index (i+4) % 8 if j = 1; which of that index's 2 slots it takes is not fixed.
All inputs are finite; a program needn't handle non-finite values.
Results may differ from the reference program's by a relative error of at most 0.001.
Values may be sent and summed in bfloat16 or wider, within the bound.
A program may use at most 128 MiB of HBM per device.

```python
import math
import jax
import jax.numpy as jnp
from jax import lax

D = 7168
FF = 2048
RANK = 128
EXP_DEV = 2
EXPERTS = 16


def draw_placement(key, part):
    key = jax.random.fold_in(key, 11)
    first_key, third_key = jax.random.split(key, 2)
    groups = EXPERTS // EXP_DEV
    values = jnp.arange(groups, dtype=jnp.int32)
    order = jax.random.permutation(first_key, groups).astype(jnp.int32)
    ranks = jnp.argsort(order).astype(jnp.int32)
    priority = jnp.where(values == 1, -2, jnp.where(values == groups // 2, -1, ranks))
    offsets = jnp.argsort(priority)[:EXP_DEV].astype(jnp.int32)
    sources = values[:, None]
    owner = (sources + offsets[None, :]) % groups
    inner_keys = jax.random.split(third_key, groups)
    inner = jax.vmap(lambda single: jax.random.permutation(single, EXP_DEV))(inner_keys).astype(jnp.int32)
    rounds = jnp.arange(EXP_DEV, dtype=jnp.int32)[None, :]
    slots = owner * EXP_DEV + inner[owner, rounds]
    return slots.reshape(-1).astype(jnp.int32)


def steps_of(own_key, dims, cuts, smallest, largest):
    level = 1.0
    for dim, shards_of in cuts:
        heights = jax.random.uniform(jax.random.fold_in(jax.random.fold_in(own_key, 6), dim), (shards_of,), jnp.float32, smallest / len(cuts), largest / len(cuts))
        level = level * jnp.repeat(jnp.exp(heights), dims[dim] // shards_of).reshape((-1,) + (1,) * (len(dims) - 1 - dim))
    return level


def noise(own_key, dims, spread, limit, cuts=(), held_as=jnp.bfloat16):
    result = spread * jax.random.normal(own_key, dims, jnp.float32)
    if cuts:
        result = result * steps_of(own_key, dims, cuts, -0.22, 0.18)
    return jnp.clip(result, -limit, limit).astype(held_as)


def setup_inputs(seed: int = 0) -> dict:
    key_list = jax.random.split(jax.random.key(seed), 5)
    gradient = noise(key_list[0], (EXPERTS, D, FF), 1.0, 6.0, ((0, 8), (1, 16)))
    momentum = noise(key_list[1], (EXPERTS, D, FF), 1.0, 6.0, ((0, 8), (1, 16)), jnp.float32)
    right_factor = noise(key_list[2], (EXPERTS, FF, RANK), 1.0, 6.0, ((0, 8),), jnp.float32)
    placement = draw_placement(jax.random.fold_in(key_list[4], 71), 0)
    return {"gradient": gradient, "momentum": momentum, "right_factor": right_factor, "placement": placement}


feedback = 0.05
epsilon = 1e-06

def single_expert(members):
    grad_block, moment_block, factor_block = members
    highest = lax.Precision.HIGHEST
    buffer = moment_block + grad_block.astype(jnp.float32)
    left_raw = jnp.dot(buffer, factor_block, precision=highest)
    gram_total = jnp.dot(left_raw.T, left_raw, precision=highest)
    triangle = jnp.linalg.cholesky(gram_total)
    left = lax.linalg.triangular_solve(triangle, left_raw, left_side=False, lower=True, transpose_a=True)
    right_full = jnp.dot(buffer.T, left, precision=highest)
    new_moment = buffer - feedback * jnp.dot(left, right_full.T, precision=highest)
    new_factor = right_full * lax.rsqrt(lax.optimization_barrier(jnp.mean(right_full * right_full, axis=0, keepdims=True)) + epsilon)
    left_scaled = (left * math.sqrt(D)).astype(jnp.bfloat16)
    return (new_moment, new_factor, left_scaled, new_factor.astype(jnp.bfloat16))

def reference(gradient, momentum, right_factor, placement):
    new_momentum, new_right, left_all, right_all = lax.map(single_expert, (gradient, momentum, right_factor))
    left_at_owner = jnp.zeros_like(left_all).at[placement].set(left_all)
    right_at_owner = jnp.zeros_like(right_all).at[placement].set(right_all)
    return (new_momentum, new_right, left_at_owner, right_at_owner)
```

```python
import functools
import math

import jax
import jax.numpy as jnp
from jax import lax
from jax.experimental import pallas as pl
from jax.experimental.pallas import tpu as pltpu
from jax.sharding import PartitionSpec as P

D = 7168
FEEDBACK = 0.05
EPSILON = 1e-06

EXPERTS_HERE = 2
ROWS = 448
FF = 2048
RANK = 128
SIDE = 4
PEERS = SIDE * SIDE
GROUPS = 8
PARTS = 2
PART_ROWS = ROWS // PARTS
BLOCK = 8
MESH = pl.DeviceIdType.MESH
F32 = jnp.float32
BF16 = jnp.bfloat16


def split(value):
    high = value.astype(BF16)
    return high, (value - high.astype(F32)).astype(BF16)


def dot(a, b):
    return jnp.dot(a, b, preferred_element_type=F32)


def dot_over_rows(a, b):
    return lax.dot_general(a, b, (((0,), (0,)), ((), ())), preferred_element_type=F32)


def factor_block(work, step):
    base = step * BLOCK
    line = lax.broadcasted_iota(jnp.int32, (BLOCK, 1), 0)
    for e in range(EXPERTS_HERE):
        rows = work[e, base : base + BLOCK, :]
        columns = [
            jnp.broadcast_to(rows[:, base + j : base + j + 1], (BLOCK, RANK)) for j in range(BLOCK)
        ]
        for j in range(BLOCK):
            inverse = lax.rsqrt(columns[j][j : j + 1, :])
            scaled = columns[j] * inverse
            below = jnp.where(line > j, scaled, 0.0)
            pivot_row = rows[j : j + 1, :] * jnp.concatenate([inverse, inverse], axis=1)
            below_wide = jnp.concatenate([below, below], axis=1)
            rows = jnp.where(line == j, pivot_row, rows - below_wide * pivot_row)
            for k in range(j + 1, BLOCK):
                columns[k] = columns[k] - below * scaled[k : k + 1, :]
        work[e, base : base + BLOCK, :] = rows
        done = base + BLOCK
        if done < RANK:
            upper = rows[:, :RANK]
            h = upper.astype(BF16).astype(F32)
            m = (upper - h).astype(BF16).astype(F32)
            l = upper - h - m
            hw = rows.astype(BF16).astype(F32)
            mw = (rows - hw).astype(BF16).astype(F32)
            lw = rows - hw - mw
            one = jnp.concatenate([h, h, m, h, m, l], axis=0).astype(BF16)
            two = jnp.concatenate([hw, mw, hw, lw, mw, hw], axis=0).astype(BF16)
            change = dot_over_rows(one, two)
            work[e, done:, :] = work[e, done:, :] - change[done:, :]


def stacked(inverse):
    high, low = split(jnp.transpose(inverse))
    wide = jnp.concatenate([high, low], axis=1)
    return jnp.concatenate([wide, wide], axis=0)


def times(value, stack):
    high, low = split(value)
    both = dot(jnp.concatenate([high, low], axis=1), stack)
    return both[:, :RANK] + both[:, RANK:]


def exchange_kernel(
    grad_hbm,
    moment_hbm,
    factor_hbm,
    buffer,
    left_out,
    right_all,
    scale_out,
    left_got,
    right_got,
    grad,
    moment,
    factor,
    high_part,
    low_part,
    raw,
    raw_cat,
    cross,
    got_one,
    sums,
    got_two,
    gram,
    gram_got,
    gram_all,
    work,
    norms,
    norms_got,
    left_send,
    right_send,
    load_sem,
    one_send,
    one_recv,
    two_send,
    two_recv,
    gram_send,
    gram_recv,
    all_send,
    all_recv,
    norm_send,
    norm_recv,
    ag_send,
    ag_recv,
    fan_send,
    fan_recv,
    own_send,
    own_recv,
):
    place = lax.axis_index("fsdp")
    group = lax.axis_index("expert")
    x = lax.rem(place, SIDE)
    y = lax.div(place, SIDE)

    def spot(shift):
        return lax.rem(place + shift, PEERS)

    def at_fsdp(index):
        return {"fsdp": index, "expert": group}

    def at_expert(shift):
        return {"fsdp": place, "expert": lax.rem(group + shift, GROUPS)}

    def shifted(v, d):
        return lax.rem(v + d, SIDE)

    first = (x, y)
    second = (y, x)

    def first_peer(e, index):
        return at_fsdp(y * SIDE + index if e == 0 else index * SIDE + x)

    def second_peer(e, index):
        return at_fsdp(index * SIDE + x if e == 0 else y * SIDE + index)

    barrier = pltpu.get_barrier_semaphore()
    for d in range(1, PEERS):
        pl.semaphore_signal(barrier, inc=1, device_id=at_fsdp(spot(d)), device_id_type=MESH)
    for d in (1, 4, GROUPS - 1):
        pl.semaphore_signal(barrier, inc=1, device_id=at_expert(d), device_id_type=MESH)

    loads = {}
    for e in range(EXPERTS_HERE):
        copy = pltpu.make_async_copy(factor_hbm.at[e], factor.at[e], load_sem.at[e, 2 * PARTS])
        copy.start()
        loads[e, 2 * PARTS] = copy
        for p in range(PARTS):
            rows = pl.ds(p * PART_ROWS, PART_ROWS)
            for k, (source, target) in enumerate(((grad_hbm, grad), (moment_hbm, moment))):
                copy = pltpu.make_async_copy(
                    source.at[e, rows], target.at[e, rows], load_sem.at[e, 2 * p + k]
                )
                copy.start()
                loads[e, 2 * p + k] = copy

    pl.semaphore_wait(barrier, PEERS - 1 + 3)

    def columns_of(e, a, b):
        return b * SIDE + a if e == 0 else a * SIDE + b

    def first_half(e):
        loads[e, 2 * PARTS].wait()
        high, low = split(factor[e])
        weights = jnp.concatenate([high, low], axis=1)
        for p in range(PARTS):
            loads[e, 2 * p].wait()
            loads[e, 2 * p + 1].wait()
            rows = slice(p * PART_ROWS, (p + 1) * PART_ROWS)
            total = moment[e, rows, :] + grad[e, rows, :].astype(F32)
            buffer[e, rows, :] = total
            bh, bl = split(total)
            for s in range(PEERS):
                high_part[e, s, rows, :] = bh[:, s * RANK : (s + 1) * RANK]
                low_part[e, s, rows, :] = bl[:, s * RANK : (s + 1) * RANK]
            product = dot(jnp.concatenate([bh, bl], axis=0), weights)
            product = product[:PART_ROWS] + product[PART_ROWS:]
            raw[e, rows, :] = product[:, :RANK] + product[:, RANK:]
        lh, ll = split(raw[e])
        raw_cat[e] = jnp.concatenate([lh, ll], axis=1)

    def gram_of(e):
        four = dot_over_rows(raw_cat[e], raw_cat[e])
        value = four[:RANK, :RANK] + four[:RANK, RANK:] + (four[RANK:, :RANK] + four[RANK:, RANK:])
        for p in range(PEERS):
            gram[p, e] = value[p * BLOCK : (p + 1) * BLOCK, :]

    sends = []

    def cross_of(e):
        for d in (2, 1, 3, 0):
            a = shifted(first[e], d)
            for pair in range(SIDE // 2):
                b0 = 2 * pair
                s0, s1 = columns_of(e, a, b0), columns_of(e, a, b0 + 1)
                bh = jnp.concatenate([high_part[e, s0], high_part[e, s1]], axis=1)
                bl = jnp.concatenate([low_part[e, s0], low_part[e, s1]], axis=1)
                value = dot_over_rows(raw_cat[e], bh) + dot_over_rows(raw_cat[e], bl)
                value = value[:RANK] + value[RANK:]
                cross[e, d, b0] = value[:, :RANK]
                cross[e, d, b0 + 1] = value[:, RANK:]
            if d:
                copy = pltpu.make_async_remote_copy(
                    src_ref=cross.at[e, d],
                    dst_ref=got_one.at[e, d - 1],
                    send_sem=one_send.at[e, d - 1],
                    recv_sem=one_recv.at[e, d - 1],
                    device_id=first_peer(e, a),
                    device_id_type=MESH,
                )
                copy.start()
                sends.append(copy)
                stage_one[e].append(copy)

    stage_one = {0: [], 1: []}
    stage_two = {0: [], 1: []}

    def sum_one(e):
        for copy in stage_one[e]:
            copy.wait_recv()
        for b in range(SIDE):
            sums[e, b] = (cross[e, 0, b] + got_one[e, 0, b]) + (got_one[e, 1, b] + got_one[e, 2, b])
        for d in (2, 1, 3):
            b = shifted(second[e], d)
            copy = pltpu.make_async_remote_copy(
                src_ref=sums.at[e, b],
                dst_ref=got_two.at[e, d - 1],
                send_sem=two_send.at[e, d - 1],
                recv_sem=two_recv.at[e, d - 1],
                device_id=second_peer(e, b),
                device_id_type=MESH,
            )
            copy.start()
            sends.append(copy)
            stage_two[e].append(copy)

    def to_all(source, target, send_sem, recv_sem):
        copies = []
        for d in range(1, PEERS):
            peer = spot(d)
            copy = pltpu.make_async_remote_copy(
                src_ref=source(peer),
                dst_ref=target(d),
                send_sem=send_sem.at[d - 1],
                recv_sem=recv_sem.at[d - 1],
                device_id=at_fsdp(peer),
                device_id_type=MESH,
            )
            copy.start()
            copies.append(copy)
        sends.extend(copies)
        return copies

    first_half(0)
    gram_of(0)
    cross_of(0)
    first_half(1)
    gram_of(1)
    gram_copies = to_all(lambda p: gram.at[p], lambda d: gram_got.at[d - 1], gram_send, gram_recv)
    cross_of(1)

    for copy in gram_copies:
        copy.wait_recv()
    total = gram[place]
    for d in range(1, PEERS):
        total = total + gram_got[d - 1]
    gram_all[place] = total
    all_copies = to_all(
        lambda p: gram_all.at[place], lambda d: gram_all.at[place], all_send, all_recv
    )
    for copy in all_copies:
        copy.wait_recv()

    eye = (
        lax.broadcasted_iota(jnp.int32, (RANK, RANK), 0)
        == lax.broadcasted_iota(jnp.int32, (RANK, RANK), 1)
    ).astype(F32)
    for e in range(EXPERTS_HERE):
        for p in range(PEERS):
            work[e, p * BLOCK : (p + 1) * BLOCK, :RANK] = gram_all[p, e]
        work[e, :, RANK:] = eye
    for step in range(RANK // BLOCK):
        factor_block(work, step)
        if step == 5:
            sum_one(0)
        if step == 10:
            sum_one(1)

    stacks = [stacked(work[e, :, RANK:]) for e in range(EXPERTS_HERE)]
    last = []

    fan = {}

    def fan_out(e, b, k):
        for d in (2, 1, 3):
            copy = pltpu.make_async_remote_copy(
                src_ref=right_all.at[e, first[e], b],
                dst_ref=right_all.at[e, first[e], b],
                send_sem=fan_send.at[e, k, d - 1],
                recv_sem=fan_recv.at[e, k, d - 1],
                device_id=first_peer(e, shifted(first[e], d)),
                device_id_type=MESH,
            )
            copy.start()
            sends.append(copy)
            last.append(copy)

    around = {0: [], 1: []}
    norms[...] = jnp.zeros_like(norms)
    for e in range(EXPERTS_HERE):
        for copy in stage_two[e]:
            copy.wait_recv()
        mine = second[e]
        whole = (sums[e, mine] + got_two[e, 0]) + (got_two[e, 1] + got_two[e, 2])
        right = times(jnp.transpose(whole), stacks[e])
        right_all[e, first[e], mine] = right
        for d in (2, 1, 3):
            copy = pltpu.make_async_remote_copy(
                src_ref=right_all.at[e, first[e], mine],
                dst_ref=right_all.at[e, first[e], mine],
                send_sem=ag_send.at[e, d - 1],
                recv_sem=ag_recv.at[e, d - 1],
                device_id=second_peer(e, shifted(mine, d)),
                device_id_type=MESH,
            )
            copy.start()
            sends.append(copy)
            around[e].append((d, copy))
        fan_out(e, mine, 0)
        norms[e : e + 1, :] = jnp.sum(right * right, axis=0, keepdims=True)
    norm_copies = to_all(lambda p: norms, lambda d: norms_got.at[d - 1], norm_send, norm_recv)

    scaled = math.sqrt(D)
    owners = (1, 4)
    for e in range(EXPERTS_HERE):
        left = times(raw[e], stacks[e])
        left_out[e] = left.astype(BF16)
        left_send[e] = (left * scaled).astype(BF16)
        copy = pltpu.make_async_remote_copy(
            src_ref=left_send.at[e],
            dst_ref=left_got.at[e],
            send_sem=own_send.at[e, 0],
            recv_sem=own_recv.at[e, 0],
            device_id=at_expert(owners[e]),
            device_id_type=MESH,
        )
        copy.start()
        sends.append(copy)
        last.append(copy)

    for e in range(EXPERTS_HERE):
        for d, copy in around[e]:
            copy.wait_recv()
            fan_out(e, shifted(second[e], SIDE - d), d)

    for copy in norm_copies:
        copy.wait_recv()
    squares = norms[...]
    for d in range(1, PEERS):
        squares = squares + norms_got[d - 1]
    scale = lax.rsqrt(squares * (1.0 / FF) + EPSILON)
    scale_out[...] = scale
    for e in range(EXPERTS_HERE):
        own = right_all[e, first[e], second[e]] * scale[e : e + 1, :]
        right_send[e] = own.astype(BF16)
        copy = pltpu.make_async_remote_copy(
            src_ref=right_send.at[e],
            dst_ref=right_got.at[e],
            send_sem=own_send.at[e, 1],
            recv_sem=own_recv.at[e, 1],
            device_id=at_expert(owners[e]),
            device_id_type=MESH,
        )
        copy.start()
        sends.append(copy)
        last.append(copy)

    for copy in last:
        copy.wait_recv()
    for copy in sends:
        copy.wait_send()


def exchange(gradient, momentum, right_factor):
    dma = pltpu.SemaphoreType.DMA
    vmem = pltpu.VMEM
    n = EXPERTS_HERE
    tile = (RANK, RANK)
    return pl.pallas_call(
        exchange_kernel,
        out_shape=(
            vmem((n, ROWS, FF), F32),
            vmem((n, ROWS, RANK), BF16),
            vmem((n, SIDE, SIDE, *tile), F32),
            vmem((8, RANK), F32),
            vmem((n, ROWS, RANK), BF16),
            vmem((n, *tile), BF16),
        ),
        in_specs=[pl.BlockSpec(memory_space=pl.ANY)] * 3,
        out_specs=[pl.BlockSpec(memory_space=pltpu.VMEM)] * 6,
        scratch_shapes=[
            vmem((n, ROWS, FF), BF16),
            vmem((n, ROWS, FF), F32),
            vmem((n, FF, RANK), F32),
            vmem((n, PEERS, ROWS, RANK), BF16),
            vmem((n, PEERS, ROWS, RANK), BF16),
            vmem((n, ROWS, RANK), F32),
            vmem((n, ROWS, 2 * RANK), BF16),
            vmem((n, SIDE, SIDE, *tile), F32),
            vmem((n, SIDE - 1, SIDE, *tile), F32),
            vmem((n, SIDE, *tile), F32),
            vmem((n, SIDE - 1, *tile), F32),
            vmem((PEERS, n, BLOCK, RANK), F32),
            vmem((PEERS - 1, n, BLOCK, RANK), F32),
            vmem((PEERS, n, BLOCK, RANK), F32),
            vmem((n, RANK, 2 * RANK), F32),
            vmem((8, RANK), F32),
            vmem((PEERS - 1, 8, RANK), F32),
            vmem((n, ROWS, RANK), BF16),
            vmem((n, *tile), BF16),
            dma((n, 2 * PARTS + 1)),
            dma((n, SIDE - 1)),
            dma((n, SIDE - 1)),
            dma((n, SIDE - 1)),
            dma((n, SIDE - 1)),
            dma((PEERS - 1,)),
            dma((PEERS - 1,)),
            dma((PEERS - 1,)),
            dma((PEERS - 1,)),
            dma((PEERS - 1,)),
            dma((PEERS - 1,)),
            dma((n, SIDE - 1)),
            dma((n, SIDE - 1)),
            dma((n, SIDE, SIDE - 1)),
            dma((n, SIDE, SIDE - 1)),
            dma((n, 2)),
            dma((n, 2)),
        ],
        compiler_params=pltpu.CompilerParams(
            collective_id=0, has_side_effects=True, vmem_limit_bytes=44 * 2**20
        ),
        cost_estimate=pl.CostEstimate(
            flops=3 * 10**9, bytes_accessed=14 * 10**6, transcendentals=0
        ),
        name="exchange",
    )(gradient, momentum, right_factor)


STEP_ROWS = 112
STEPS = ROWS // STEP_ROWS


def finish_kernel(place_ref, buffer, left, right, scale, lgot, rgot, new_m, new_r, left_own, right_own):
    e = pl.program_id(0)
    step = pl.program_id(1)
    rows = pl.ds(pl.multiple_of(step * STEP_ROWS, 16), STEP_ROWS)
    factor = left[e, rows, :]

    def columns(s):
        return s * RANK, (s + 1) * RANK

    for s in range(PEERS):
        a0, b0 = s % SIDE, s // SIDE
        a = jnp.where(e == 0, a0, b0)
        b = jnp.where(e == 0, b0, a0)
        block = right[e, a, b]
        part = lax.dot_general(
            factor, block.astype(BF16), (((1,), (1,)), ((), ())), preferred_element_type=F32
        )
        lo, hi = columns(s)
        new_m[0, :, lo:hi] = buffer[e, rows, lo:hi] - FEEDBACK * part

    @pl.when(step == 0)
    def _():
        for s in range(PEERS):
            a0, b0 = s % SIDE, s // SIDE
            a = jnp.where(e == 0, a0, b0)
            b = jnp.where(e == 0, b0, a0)
            lo, hi = columns(s)
            new_r[0, lo:hi, :] = right[e, a, b] * scale[pl.ds(e, 1), :]

    group = lax.axis_index("expert")
    source = EXPERTS_HERE * lax.rem(group + GROUPS - 1, GROUPS)
    straight = place_ref[source] == EXPERTS_HERE * group
    pick = jnp.where(straight, e, 1 - e)

    @pl.when(step == 0)
    def _():
        left_own[0] = lgot[pick]
        right_own[0] = rgot[pick]


def finish(placement, pieces):
    n = EXPERTS_HERE
    whole = pl.BlockSpec(memory_space=pltpu.VMEM)
    return pl.pallas_call(
        finish_kernel,
        grid=(n, STEPS),
        out_shape=(
            jax.ShapeDtypeStruct((n, ROWS, FF), F32),
            jax.ShapeDtypeStruct((n, FF, RANK), F32),
            jax.ShapeDtypeStruct((n, ROWS, RANK), BF16),
            jax.ShapeDtypeStruct((n, RANK, RANK), BF16),
        ),
        in_specs=[pl.BlockSpec(memory_space=pltpu.SMEM)] + [whole] * 6,
        out_specs=(
            pl.BlockSpec((1, STEP_ROWS, FF), lambda e, i: (e, i, 0)),
            pl.BlockSpec((1, FF, RANK), lambda e, i: (e, 0, 0)),
            pl.BlockSpec((1, ROWS, RANK), lambda e, i: (e, 0, 0)),
            pl.BlockSpec((1, RANK, RANK), lambda e, i: (e, 0, 0)),
        ),
        compiler_params=pltpu.CompilerParams(vmem_limit_bytes=16 * 2**20),
        cost_estimate=pl.CostEstimate(
            flops=5 * 10**8, bytes_accessed=10 * 10**6, transcendentals=0
        ),
        name="finish",
    )(placement, *pieces)


def shards(gradient, momentum, right_factor, placement):
    pieces = exchange(gradient, momentum, right_factor)
    return finish(placement, pieces)


def solution(mesh):
    placed = (P("expert", "fsdp", None), P("expert", "fsdp", None), P("expert", None, None), P())
    return jax.shard_map(
        shards,
        mesh=mesh,
        in_specs=placed,
        out_specs=(
            P("expert", "fsdp", None),
            P("expert", None, None),
            P("expert", "fsdp", None),
            P("expert", "fsdp", None),
        ),
        check_vma=False,
    )
```

```python
import functools
import math

import jax
import jax.numpy as jnp
from jax import lax
from jax.experimental import pallas as pl
from jax.experimental.pallas import tpu as pltpu
from jax.sharding import PartitionSpec as P

D = 7168
FEEDBACK = 0.05
EPSILON = 1e-06

EXPERTS_HERE = 2
ROWS = 448
FF = 2048
RANK = 128
SIDE = 4
PEERS = SIDE * SIDE
GROUPS = 8
PARTS = 2
PART_ROWS = ROWS // PARTS
BLOCK = 8
HEAD = 16
TILE = RANK + HEAD
CHUNK = SIDE * RANK + HEAD
MESH = pl.DeviceIdType.MESH
F32 = jnp.float32
BF16 = jnp.bfloat16
CODE = jnp.int16


def split(value):
    high = value.astype(BF16)
    return high, (value - high.astype(F32)).astype(BF16)


def dot(a, b):
    return jnp.dot(a, b, preferred_element_type=F32)


def dot_last(a, b):
    return lax.dot_general(a, b, (((1,), (1,)), ((), ())), preferred_element_type=F32)


def dot_over_rows(a, b):
    return lax.dot_general(a, b, (((0,), (0,)), ((), ())), preferred_element_type=F32)


def factor_block(work, step):
    base = step * BLOCK
    line = lax.broadcasted_iota(jnp.int32, (BLOCK, 1), 0)
    for e in range(EXPERTS_HERE):
        rows = work[e, base : base + BLOCK, :]
        columns = [
            jnp.broadcast_to(rows[:, base + j : base + j + 1], (BLOCK, RANK)) for j in range(BLOCK)
        ]
        for j in range(BLOCK):
            inverse = lax.rsqrt(columns[j][j : j + 1, :])
            scaled = columns[j] * inverse
            below = jnp.where(line > j, scaled, 0.0)
            pivot_row = rows[j : j + 1, :] * jnp.concatenate([inverse, inverse], axis=1)
            below_wide = jnp.concatenate([below, below], axis=1)
            rows = jnp.where(line == j, pivot_row, rows - below_wide * pivot_row)
            for k in range(j + 1, BLOCK):
                columns[k] = columns[k] - below * scaled[k : k + 1, :]
        work[e, base : base + BLOCK, :] = rows
        done = base + BLOCK
        if done < RANK:
            upper = rows[:, :RANK]
            h = upper.astype(BF16).astype(F32)
            m = (upper - h).astype(BF16).astype(F32)
            l = upper - h - m
            hw = rows.astype(BF16).astype(F32)
            mw = (rows - hw).astype(BF16).astype(F32)
            lw = rows - hw - mw
            one = jnp.concatenate([h, h, m, h, m, l], axis=0).astype(BF16)
            two = jnp.concatenate([hw, mw, hw, lw, mw, hw], axis=0).astype(BF16)
            change = dot_over_rows(one, two)
            work[e, done:, :] = work[e, done:, :] - change[done:, :]


def stacked(inverse):
    high, low = split(jnp.transpose(inverse))
    wide = jnp.concatenate([high, low], axis=1)
    return jnp.concatenate([wide, wide], axis=0)


def times(value, stack):
    high, low = split(value)
    both = dot(jnp.concatenate([high, low], axis=1), stack)
    return both[:, :RANK] + both[:, RANK:]


def exponent_of(peak):
    peak = jnp.broadcast_to(jnp.maximum(peak, 1e-30), (HEAD, RANK))
    return jnp.ceil(jnp.log2(peak))


def coded(value, exponent):
    scaled = jnp.round(value * jnp.exp2(15.0 - exponent[:1]))
    return jnp.clip(scaled, -32767.0, 32767.0).astype(jnp.int32).astype(CODE)


def code_tile(target, value):
    exponent = exponent_of(jnp.max(jnp.abs(value), axis=0, keepdims=True))
    target[:RANK, :] = coded(value, exponent)
    target[RANK:, :] = exponent.astype(jnp.int32).astype(CODE)


def step_of(head):
    return jnp.exp2(head.astype(jnp.int32).astype(F32)[:1] - 15.0)


def number(code):
    return code.astype(jnp.int32).astype(F32)


def exchange_kernel(
    grad_hbm,
    moment_hbm,
    factor_hbm,
    buffer,
    new_right,
    left_got,
    right_got,
    grad,
    moment,
    factor,
    high_part,
    low_part,
    raw,
    turned,
    cross,
    own_one,
    got_one,
    sums,
    got_two,
    whole,
    wire,
    gram,
    gram_got,
    gram_all,
    work,
    norms,
    left,
    left_send,
    right_send,
    load_sem,
    one_send,
    one_recv,
    two_send,
    two_recv,
    gram_send,
    gram_recv,
    all_send,
    all_recv,
    norm_send,
    norm_recv,
    ag_send,
    ag_recv,
    fan_send,
    fan_recv,
    own_send,
    own_recv,
):
    place = lax.axis_index("fsdp")
    group = lax.axis_index("expert")
    x = lax.rem(place, SIDE)
    y = lax.div(place, SIDE)

    def spot(shift):
        return lax.rem(place + shift, PEERS)

    def at_fsdp(index):
        return {"fsdp": index, "expert": group}

    def at_expert(shift):
        return {"fsdp": place, "expert": lax.rem(group + shift, GROUPS)}

    def shifted(v, d):
        return lax.rem(v + d, SIDE)

    first = (x, y)
    second = (y, x)

    def first_peer(e, index):
        return at_fsdp(y * SIDE + index if e == 0 else index * SIDE + x)

    def second_peer(e, index):
        return at_fsdp(index * SIDE + x if e == 0 else y * SIDE + index)

    def columns_of(e, a, b):
        return b * SIDE + a if e == 0 else a * SIDE + b

    barrier = pltpu.get_barrier_semaphore()
    for d in range(1, PEERS):
        pl.semaphore_signal(barrier, inc=1, device_id=at_fsdp(spot(d)), device_id_type=MESH)
    for d in (1, 4, GROUPS - 1):
        pl.semaphore_signal(barrier, inc=1, device_id=at_expert(d), device_id_type=MESH)

    loads = {}
    for e in range(EXPERTS_HERE):
        copy = pltpu.make_async_copy(factor_hbm.at[e], factor.at[e], load_sem.at[e, 2 * PARTS])
        copy.start()
        loads[e, 2 * PARTS] = copy
        for p in range(PARTS):
            rows = pl.ds(p * PART_ROWS, PART_ROWS)
            for k, (source, target) in enumerate(((grad_hbm, grad), (moment_hbm, moment))):
                copy = pltpu.make_async_copy(
                    source.at[e, rows], target.at[e, rows], load_sem.at[e, 2 * p + k]
                )
                copy.start()
                loads[e, 2 * p + k] = copy

    sends = []
    last = []

    def send(source, target, send_sem, recv_sem, peer):
        copy = pltpu.make_async_remote_copy(
            src_ref=source,
            dst_ref=target,
            send_sem=send_sem,
            recv_sem=recv_sem,
            device_id=peer,
            device_id_type=MESH,
        )
        copy.start()
        sends.append(copy)
        return copy

    def to_all(source, target, send_sem, recv_sem):
        copies = []
        for d in range(1, PEERS):
            peer = spot(d)
            copies.append(
                send(source(peer), target(d), send_sem.at[d - 1], recv_sem.at[d - 1], at_fsdp(peer))
            )
        return copies

    def first_half(e):
        loads[e, 2 * PARTS].wait()
        value = factor[e]
        norm = jnp.sum(value * value, axis=0, keepdims=True)
        high, low = split(value * lax.rsqrt(jnp.maximum(norm, 1e-30)))
        weights = jnp.concatenate([high, low], axis=1)
        for p in range(PARTS):
            loads[e, 2 * p].wait()
            loads[e, 2 * p + 1].wait()
            rows = slice(p * PART_ROWS, (p + 1) * PART_ROWS)
            total = moment[e, rows, :] + grad[e, rows, :].astype(F32)
            buffer[e, rows, :] = total
            bh, bl = split(total)
            for s in range(PEERS):
                high_part[e, s, rows, :] = bh[:, s * RANK : (s + 1) * RANK]
                low_part[e, s, rows, :] = bl[:, s * RANK : (s + 1) * RANK]
            product = dot(jnp.concatenate([bh, bl], axis=0), weights)
            product = product[:PART_ROWS] + product[PART_ROWS:]
            raw[e, rows, :] = product[:, :RANK] + product[:, RANK:]
        lh, ll = split(raw[e])
        th, tl = split(jnp.transpose(raw[e]))
        turned[e] = jnp.concatenate([th, tl], axis=0)
        four = dot(turned[e], jnp.concatenate([lh, ll], axis=1))
        value = four[:RANK, :RANK] + four[:RANK, RANK:] + (four[RANK:, :RANK] + four[RANK:, RANK:])
        for p in range(PEERS):
            gram[p, e] = value[p * BLOCK : (p + 1) * BLOCK, :]

    def cross_of(e, d):
        a = shifted(first[e], d)
        pairs = []
        for b in range(0, SIDE, 2):
            s0, s1 = columns_of(e, a, b), columns_of(e, a, b + 1)
            bh = jnp.concatenate([high_part[e, s0], high_part[e, s1]], axis=1)
            bl = jnp.concatenate([low_part[e, s0], low_part[e, s1]], axis=1)
            value = dot(turned[e], bh) + dot(turned[e], bl)
            pairs.append(value[:RANK] + value[RANK:])
        if d == 0:
            for b in range(SIDE):
                own_one[e, b] = pairs[b // 2][:, (b % 2) * RANK : (b % 2 + 1) * RANK]
            return
        peak = jnp.maximum(
            *[jnp.max(jnp.abs(value), axis=0, keepdims=True) for value in pairs]
        )
        exponent = exponent_of(jnp.maximum(peak[:, :RANK], peak[:, RANK:]))
        for b in range(SIDE):
            value = pairs[b // 2][:, (b % 2) * RANK : (b % 2 + 1) * RANK]
            cross[e, d - 1, b * RANK : (b + 1) * RANK, :] = coded(value, exponent)
        cross[e, d - 1, SIDE * RANK :, :] = exponent.astype(jnp.int32).astype(CODE)

    def send_one(e, d):
        return send(
            cross.at[e, d - 1],
            got_one.at[e, d - 1],
            one_send.at[e, d - 1],
            one_recv.at[e, d - 1],
            first_peer(e, shifted(first[e], d)),
        )

    def sum_one(e):
        for copy in stage_one[e]:
            copy.wait_recv()
        steps = [step_of(got_one[e, k, SIDE * RANK :, :]) for k in range(SIDE - 1)]
        copies = []
        for d in (2, 1, 3, 0):
            b = shifted(second[e], d)
            rows = pl.ds(pl.multiple_of(b * RANK, RANK), RANK)
            value = own_one[e, b]
            for k in range(SIDE - 1):
                value = value + number(got_one[e, k, rows, :]) * steps[k]
            if d == 0:
                whole[e] = value
                continue
            code_tile(sums.at[e, d - 1], value)
            copies.append(
                send(
                    sums.at[e, d - 1],
                    got_two.at[e, d - 1],
                    two_send.at[e, d - 1],
                    two_recv.at[e, d - 1],
                    second_peer(e, b),
                )
            )
        return copies

    def fan_out(e, b, k):
        for d in (2, 1, 3):
            tile = wire.at[e, first[e], b]
            copy = send(
                tile,
                tile,
                fan_send.at[e, k, d - 1],
                fan_recv.at[e, k, d - 1],
                first_peer(e, shifted(first[e], d)),
            )
            fans[e, k, d] = copy

    def sum_two(e):
        for copy in stage_two[e]:
            copy.wait_recv()
        value = whole[e]
        for k in range(SIDE - 1):
            value = value + number(got_two[e, k, :RANK, :]) * step_of(got_two[e, k, RANK:, :])
        value = jnp.transpose(value)
        whole[e] = value
        mine = second[e]
        tile = wire.at[e, first[e], mine]
        code_tile(tile, value)
        for d in (2, 1, 3):
            around[e, d] = send(
                tile,
                tile,
                ag_send.at[e, d - 1],
                ag_recv.at[e, d - 1],
                second_peer(e, shifted(mine, d)),
            )
        fan_out(e, mine, 0)

    def forward(e):
        for d in (1, 3, 2):
            around[e, d].wait_recv()
            fan_out(e, shifted(second[e], SIDE - d), d)

    stage_one = {}
    stage_two = {}
    around = {}
    fans = {}

    first_half(0)
    for d in (2, 1, 3):
        cross_of(0, d)
    pl.semaphore_wait(barrier, PEERS - 1 + 3)
    stage_one[0] = [send_one(0, d) for d in (2, 1, 3)]
    first_half(1)
    gram_copies = to_all(lambda p: gram.at[p], lambda d: gram_got.at[d - 1], gram_send, gram_recv)
    stage_one[1] = []
    for d in (2, 1, 3):
        cross_of(1, d)
        stage_one[1].append(send_one(1, d))
    cross_of(0, 0)
    cross_of(1, 0)

    for copy in gram_copies:
        copy.wait_recv()
    total = gram[place]
    for d in range(1, PEERS):
        total = total + gram_got[d - 1]
    gram_all[place] = total
    all_copies = to_all(
        lambda p: gram_all.at[place], lambda d: gram_all.at[place], all_send, all_recv
    )
    stage_two[0] = sum_one(0)
    for copy in all_copies:
        copy.wait_recv()

    eye = (
        lax.broadcasted_iota(jnp.int32, (RANK, RANK), 0)
        == lax.broadcasted_iota(jnp.int32, (RANK, RANK), 1)
    ).astype(F32)
    for e in range(EXPERTS_HERE):
        for p in range(PEERS):
            work[e, p * BLOCK : (p + 1) * BLOCK, :RANK] = gram_all[p, e]
        work[e, :, RANK:] = eye
    for step in range(RANK // BLOCK):
        factor_block(work, step)
        if step == 4:
            stage_two[1] = sum_one(1)
        if step == 8:
            sum_two(0)
        if step == 13:
            sum_two(1)

    stacks = [stacked(work[e, :, RANK:]) for e in range(EXPERTS_HERE)]

    norms[place] = jnp.zeros((8, RANK), F32)
    rights = []
    for e in range(EXPERTS_HERE):
        right = times(whole[e], stacks[e])
        rights.append(right)
        norms[place, e : e + 1, :] = jnp.sum(right * right, axis=0, keepdims=True)
    norm_copies = to_all(lambda p: norms.at[place], lambda d: norms.at[place], norm_send, norm_recv)
    forward(0)
    forward(1)

    owners = (1, 4)
    for e in range(EXPERTS_HERE):
        value = times(raw[e], stacks[e])
        left[e] = value.astype(BF16)
        left_send[e] = (value * math.sqrt(D)).astype(BF16)
        last.append(
            send(
                left_send.at[e],
                left_got.at[e],
                own_send.at[e, 0],
                own_recv.at[e, 0],
                at_expert(owners[e]),
            )
        )

    for copy in norm_copies:
        copy.wait_recv()
    squares = norms[0]
    for p in range(1, PEERS):
        squares = squares + norms[p]
    scale = lax.rsqrt(squares * (1.0 / FF) + EPSILON)
    for e in range(EXPERTS_HERE):
        right_send[e] = (rights[e] * scale[e : e + 1, :]).astype(BF16)
        last.append(
            send(
                right_send.at[e],
                right_got.at[e],
                own_send.at[e, 1],
                own_recv.at[e, 1],
                at_expert(owners[e]),
            )
        )

    order = [(0, 0), (1, 0), (3, 0), (2, 0)] + [(k, d) for k in (0, 1, 3, 2) for d in (1, 3, 2)]
    for pair in range(0, PEERS, 2):
        for e in range(EXPERTS_HERE):
            values = []
            for k, d in order[pair : pair + 2]:
                if d:
                    fans[e, k, d].wait_recv()
                a = shifted(first[e], SIDE - d) if d else first[e]
                b = shifted(second[e], SIDE - k) if k else second[e]
                code = wire[e, a, b, :RANK, :]
                values.append(number(code) * step_of(wire[e, a, b, RANK:, :]))
            right = times(jnp.concatenate(values, axis=0), stacks[e])
            part = dot_last(left[e], (right * FEEDBACK).astype(BF16))
            right = right * scale[e : e + 1, :]
            for i, (k, d) in enumerate(order[pair : pair + 2]):
                a = shifted(first[e], SIDE - d) if d else first[e]
                b = shifted(second[e], SIDE - k) if k else second[e]
                span = pl.ds(pl.multiple_of(columns_of(e, a, b) * RANK, RANK), RANK)
                new_right[e, span, :] = right[i * RANK : (i + 1) * RANK]
                buffer[e, :, span] = buffer[e, :, span] - part[:, i * RANK : (i + 1) * RANK]

    for copy in last:
        copy.wait_recv()
    for copy in sends:
        copy.wait_send()


def exchange(gradient, momentum, right_factor):
    dma = pltpu.SemaphoreType.DMA
    vmem = pltpu.VMEM
    n = EXPERTS_HERE
    tile = (RANK, RANK)
    others = SIDE - 1
    return pl.pallas_call(
        exchange_kernel,
        out_shape=(
            vmem((n, ROWS, FF), F32),
            vmem((n, FF, RANK), F32),
            vmem((n, ROWS, RANK), BF16),
            vmem((n, *tile), BF16),
        ),
        in_specs=[pl.BlockSpec(memory_space=pl.ANY)] * 3,
        out_specs=[pl.BlockSpec(memory_space=pltpu.VMEM)] * 4,
        scratch_shapes=[
            vmem((n, ROWS, FF), BF16),
            vmem((n, ROWS, FF), F32),
            vmem((n, FF, RANK), F32),
            vmem((n, PEERS, ROWS, RANK), BF16),
            vmem((n, PEERS, ROWS, RANK), BF16),
            vmem((n, ROWS, RANK), F32),
            vmem((n, 2 * RANK, ROWS), BF16),
            vmem((n, others, CHUNK, RANK), CODE),
            vmem((n, SIDE, *tile), F32),
            vmem((n, others, CHUNK, RANK), CODE),
            vmem((n, others, TILE, RANK), CODE),
            vmem((n, others, TILE, RANK), CODE),
            vmem((n, *tile), F32),
            vmem((n, SIDE, SIDE, TILE, RANK), CODE),
            vmem((PEERS, n, BLOCK, RANK), F32),
            vmem((PEERS - 1, n, BLOCK, RANK), F32),
            vmem((PEERS, n, BLOCK, RANK), F32),
            vmem((n, RANK, 2 * RANK), F32),
            vmem((PEERS, 8, RANK), F32),
            vmem((n, ROWS, RANK), BF16),
            vmem((n, ROWS, RANK), BF16),
            vmem((n, *tile), BF16),
            dma((n, 2 * PARTS + 1)),
            dma((n, others)),
            dma((n, others)),
            dma((n, others)),
            dma((n, others)),
            dma((PEERS - 1,)),
            dma((PEERS - 1,)),
            dma((PEERS - 1,)),
            dma((PEERS - 1,)),
            dma((PEERS - 1,)),
            dma((PEERS - 1,)),
            dma((n, others)),
            dma((n, others)),
            dma((n, SIDE, others)),
            dma((n, SIDE, others)),
            dma((n, 2)),
            dma((n, 2)),
        ],
        compiler_params=pltpu.CompilerParams(
            collective_id=0, has_side_effects=True, vmem_limit_bytes=44 * 2**20
        ),
        cost_estimate=pl.CostEstimate(
            flops=3 * 10**9, bytes_accessed=14 * 10**6, transcendentals=0
        ),
        name="exchange",
    )(gradient, momentum, right_factor)


STORES = 4
STORE_ROWS = ROWS // STORES


def store_kernel(place_ref, new_m, new_r, lgot, rgot, m_out, r_out, left_out, right_out, sem):
    group = lax.axis_index("expert")
    source = EXPERTS_HERE * lax.rem(group + GROUPS - 1, GROUPS)
    straight = place_ref[source] == EXPERTS_HERE * group
    copies = []
    for e in range(EXPERTS_HERE):
        for p in range(STORES):
            rows = pl.ds(p * STORE_ROWS, STORE_ROWS)
            copies.append((new_m.at[e, rows], m_out.at[e, rows]))
        copies.append((new_r.at[e], r_out.at[e]))
    for e in range(EXPERTS_HERE):
        pick = jnp.where(straight, e, 1 - e)
        copies.append((lgot.at[pick], left_out.at[e]))
        copies.append((rgot.at[pick], right_out.at[e]))
    started = []
    for k, (a, b) in enumerate(copies):
        copy = pltpu.make_async_copy(a, b, sem.at[k])
        copy.start()
        started.append(copy)
    for copy in started:
        copy.wait()


def store(placement, pieces):
    n = EXPERTS_HERE
    return pl.pallas_call(
        store_kernel,
        out_shape=(
            jax.ShapeDtypeStruct((n, ROWS, FF), F32),
            jax.ShapeDtypeStruct((n, FF, RANK), F32),
            jax.ShapeDtypeStruct((n, ROWS, RANK), BF16),
            jax.ShapeDtypeStruct((n, RANK, RANK), BF16),
        ),
        in_specs=[pl.BlockSpec(memory_space=pltpu.SMEM)]
        + [pl.BlockSpec(memory_space=pltpu.VMEM)] * 4,
        out_specs=[pl.BlockSpec(memory_space=pl.ANY)] * 4,
        scratch_shapes=[pltpu.SemaphoreType.DMA((n * (STORES + 3),))],
        compiler_params=pltpu.CompilerParams(vmem_limit_bytes=16 * 2**20),
        cost_estimate=pl.CostEstimate(flops=0, bytes_accessed=10 * 10**6, transcendentals=0),
        name="store",
    )(placement, *pieces)


def shards(gradient, momentum, right_factor, placement):
    pieces = exchange(gradient, momentum, right_factor)
    return store(placement, pieces)


def solution(mesh):
    placed = (P("expert", "fsdp", None), P("expert", "fsdp", None), P("expert", None, None), P())
    return jax.shard_map(
        shards,
        mesh=mesh,
        in_specs=placed,
        out_specs=(
            P("expert", "fsdp", None),
            P("expert", None, None),
            P("expert", "fsdp", None),
            P("expert", "fsdp", None),
        ),
        check_vma=False,
    )
```

```python
import functools
import math

import jax
import jax.numpy as jnp
from jax import lax
from jax.experimental import pallas as pl
from jax.experimental.pallas import tpu as pltpu
from jax.sharding import PartitionSpec as P

D = 7168
FEEDBACK = 0.05
EPSILON = 1e-06

EXPERTS_HERE = 2
ROWS = 448
FF = 2048
RANK = 128
SIDE = 4
PEERS = SIDE * SIDE
GROUPS = 8
PARTS = 2
PART_ROWS = ROWS // PARTS
BLOCK = 8
HEAD = 16
TILE = RANK + HEAD
CHUNK = SIDE * RANK + HEAD
ORDER = (2, 1, 3, 0)
QUARTER = RANK // SIDE
MESH = pl.DeviceIdType.MESH
F32 = jnp.float32
BF16 = jnp.bfloat16
CODE = jnp.int16


def split(value):
    high = value.astype(BF16)
    return high, (value - high.astype(F32)).astype(BF16)


def dot(a, b):
    return jnp.dot(a, b, preferred_element_type=F32)


def dot_last(a, b):
    return lax.dot_general(a, b, (((1,), (1,)), ((), ())), preferred_element_type=F32)


def dot_over_rows(a, b):
    return lax.dot_general(a, b, (((0,), (0,)), ((), ())), preferred_element_type=F32)


def factor_block(work, step):
    base = step * BLOCK
    line = lax.broadcasted_iota(jnp.int32, (BLOCK, 1), 0)
    for e in range(EXPERTS_HERE):
        rows = work[e, base : base + BLOCK, :]
        columns = [
            jnp.broadcast_to(rows[:, base + j : base + j + 1], (BLOCK, RANK)) for j in range(BLOCK)
        ]
        for j in range(BLOCK):
            inverse = lax.rsqrt(columns[j][j : j + 1, :])
            scaled = columns[j] * inverse
            below = jnp.where(line > j, scaled, 0.0)
            pivot_row = rows[j : j + 1, :] * jnp.concatenate([inverse, inverse], axis=1)
            below_wide = jnp.concatenate([below, below], axis=1)
            rows = jnp.where(line == j, pivot_row, rows - below_wide * pivot_row)
            for k in range(j + 1, BLOCK):
                columns[k] = columns[k] - below * scaled[k : k + 1, :]
        work[e, base : base + BLOCK, :] = rows
        done = base + BLOCK
        if done < RANK:
            upper = rows[:, :RANK]
            h = upper.astype(BF16).astype(F32)
            m = (upper - h).astype(BF16).astype(F32)
            l = upper - h - m
            hw = rows.astype(BF16).astype(F32)
            mw = (rows - hw).astype(BF16).astype(F32)
            lw = rows - hw - mw
            one = jnp.concatenate([h, h, m, h, m, l], axis=0).astype(BF16)
            two = jnp.concatenate([hw, mw, hw, lw, mw, hw], axis=0).astype(BF16)
            change = dot_over_rows(one, two)
            work[e, done:, :] = work[e, done:, :] - change[done:, :]


def stacked(inverse):
    high, low = split(jnp.transpose(inverse))
    wide = jnp.concatenate([high, low], axis=1)
    return jnp.concatenate([wide, wide], axis=0)


def times(value, stack):
    high, low = split(value)
    both = dot(jnp.concatenate([high, low], axis=1), stack)
    return both[:, :RANK] + both[:, RANK:]


def exponent_of(peak):
    peak = jnp.broadcast_to(jnp.maximum(peak, 1e-30), (HEAD, RANK))
    return jnp.ceil(jnp.log2(peak))


def coded(value, exponent):
    scaled = jnp.round(value * jnp.exp2(15.0 - exponent[:1]))
    return jnp.clip(scaled, -32767.0, 32767.0).astype(jnp.int32).astype(CODE)


def code_tile(target, value):
    exponent = exponent_of(jnp.max(jnp.abs(value), axis=0, keepdims=True))
    target[:RANK, :] = coded(value, exponent)
    target[RANK:, :] = exponent.astype(jnp.int32).astype(CODE)


def step_of(head):
    return jnp.exp2(head.astype(jnp.int32).astype(F32)[:1] - 15.0)


def number(code):
    return code.astype(jnp.int32).astype(F32)


def exchange_kernel(
    grad_hbm,
    moment_hbm,
    factor_hbm,
    buffer,
    new_right,
    left_got,
    right_got,
    grad,
    moment,
    factor,
    high_part,
    low_part,
    raw,
    turned,
    cross,
    own_one,
    got_one,
    sums,
    got_two,
    whole,
    wire,
    gram,
    gram_one,
    gram_two,
    gram_all,
    work,
    squares,
    left,
    left_send,
    right_send,
    load_sem,
    one_send,
    one_recv,
    two_send,
    two_recv,
    gram_send,
    gram_recv,
    ag_send,
    ag_recv,
    fan_send,
    fan_recv,
    own_send,
    own_recv,
):
    place = lax.axis_index("fsdp")
    group = lax.axis_index("expert")
    x = lax.rem(place, SIDE)
    y = lax.div(place, SIDE)

    def along_x(index):
        return {"fsdp": y * SIDE + index, "expert": group}

    def along_y(index):
        return {"fsdp": index * SIDE + x, "expert": group}

    def at_expert(shift):
        return {"fsdp": place, "expert": lax.rem(group + shift, GROUPS)}

    def shifted(v, d):
        return lax.rem(v + d, SIDE)

    first = (x, y)
    second = (y, x)

    def first_peer(e, index):
        return along_x(index) if e == 0 else along_y(index)

    def second_peer(e, index):
        return along_y(index) if e == 0 else along_x(index)

    def columns_of(e, a, b):
        return b * SIDE + a if e == 0 else a * SIDE + b

    barrier = pltpu.get_barrier_semaphore()
    for d in range(1, SIDE):
        for peer in (along_x(shifted(x, d)), along_y(shifted(y, d))):
            pl.semaphore_signal(barrier, inc=1, device_id=peer, device_id_type=MESH)
    for d in (1, 4, GROUPS - 1):
        pl.semaphore_signal(barrier, inc=1, device_id=at_expert(d), device_id_type=MESH)

    loads = {}

    def load(e, p):
        if p == PARTS:
            pieces = ((factor_hbm.at[e], factor.at[e]),)
        else:
            rows = pl.ds(p * PART_ROWS, PART_ROWS)
            pieces = (
                (grad_hbm.at[e, rows], grad.at[e, rows]),
                (moment_hbm.at[e, rows], moment.at[e, rows]),
            )
        for k, (source, target) in enumerate(pieces):
            copy = pltpu.make_async_copy(source, target, load_sem.at[e, 2 * p + k])
            copy.start()
            loads[e, 2 * p + k] = copy

    load(0, PARTS)
    for p in range(PARTS):
        load(0, p)

    sends = []
    last = []

    def send(source, target, send_sem, recv_sem, peer):
        copy = pltpu.make_async_remote_copy(
            src_ref=source,
            dst_ref=target,
            send_sem=send_sem,
            recv_sem=recv_sem,
            device_id=peer,
            device_id_type=MESH,
        )
        copy.start()
        sends.append(copy)
        return copy

    def total_of(slots):
        return (slots(0) + slots(1)) + (slots(2) + slots(3))

    def to_column(source, target, send_sems, recv_sems):
        return [
            send(
                source(shifted(y, d)),
                target,
                send_sems.at[d - 1],
                recv_sems.at[d - 1],
                along_y(shifted(y, d)),
            )
            for d in (2, 1, 3)
        ]

    def to_row(slot, send_sems, recv_sems):
        return [
            send(slot, slot, send_sems.at[d - 1], recv_sems.at[d - 1], along_x(shifted(x, d)))
            for d in (2, 1, 3)
        ]

    def first_half(e):
        loads[e, 2 * PARTS].wait()
        if e == 0:
            load(1, PARTS)
        value = factor[e]
        norm = jnp.sum(value * value, axis=0, keepdims=True)
        high, low = split(value * lax.rsqrt(jnp.maximum(norm, 1e-30)))
        weights = jnp.concatenate([high, low], axis=1)
        for p in range(PARTS):
            loads[e, 2 * p].wait()
            loads[e, 2 * p + 1].wait()
            if e == 0:
                load(1, p)
            rows = slice(p * PART_ROWS, (p + 1) * PART_ROWS)
            total = moment[e, rows, :] + grad[e, rows, :].astype(F32)
            buffer[e, rows, :] = total
            bh, bl = split(total)
            for s in range(PEERS):
                high_part[e, s, rows, :] = bh[:, s * RANK : (s + 1) * RANK]
                low_part[e, s, rows, :] = bl[:, s * RANK : (s + 1) * RANK]
            product = dot(bh, weights)
            raw[e, rows, :] = product[:, :RANK] + (product[:, RANK:] + dot(bl, high))
        lh, ll = split(raw[e])
        th, tl = split(jnp.transpose(raw[e]))
        turned[e] = jnp.concatenate([th, tl], axis=0)
        four = dot(turned[e], jnp.concatenate([lh, ll], axis=1))
        value = four[:RANK, :RANK] + four[:RANK, RANK:] + (four[RANK:, :RANK] + four[RANK:, RANK:])
        for q in range(SIDE):
            gram[q, e] = value[q * QUARTER : (q + 1) * QUARTER, :]

    def cross_of(e, d):
        a = shifted(first[e], d)
        pairs = []
        for k0, k1 in ((ORDER[0], ORDER[1]), (ORDER[2], ORDER[3])):
            s0 = columns_of(e, a, shifted(second[e], k0))
            s1 = columns_of(e, a, shifted(second[e], k1))
            bh = jnp.concatenate([high_part[e, s0], high_part[e, s1]], axis=1)
            bl = jnp.concatenate([low_part[e, s0], low_part[e, s1]], axis=1)
            value = dot(turned[e], bh)
            pairs.append(value[:RANK] + (value[RANK:] + dot(turned[e, :RANK, :], bl)))
        tiles = [pairs[g // 2][:, (g % 2) * RANK : (g % 2 + 1) * RANK] for g in range(SIDE)]
        if d == 0:
            for g in range(SIDE):
                own_one[e, g] = tiles[g]
            return
        peak = jnp.maximum(*[jnp.max(jnp.abs(value), axis=0, keepdims=True) for value in pairs])
        exponent = exponent_of(jnp.maximum(peak[:, :RANK], peak[:, RANK:]))
        cross[e, d - 1, :HEAD, :] = exponent.astype(jnp.int32).astype(CODE)
        for g in range(SIDE):
            cross[e, d - 1, HEAD + g * RANK : HEAD + (g + 1) * RANK, :] = coded(tiles[g], exponent)

    def send_one(e):
        for g in range(SIDE):
            start, end = (HEAD + g * RANK if g else 0), HEAD + (g + 1) * RANK
            for d in (2, 1, 3):
                stage_one[e, g, d] = send(
                    cross.at[e, d - 1, start:end],
                    got_one.at[e, d - 1, start:end],
                    one_send.at[e, g, d - 1],
                    one_recv.at[e, g, d - 1],
                    first_peer(e, shifted(first[e], d)),
                )

    def sum_one(e, g):
        for d in (2, 1, 3):
            stage_one[e, g, d].wait_recv()
        value = own_one[e, g]
        for k in range(SIDE - 1):
            step = step_of(got_one[e, k, :HEAD, :])
            value = value + number(got_one[e, k, HEAD + g * RANK : HEAD + (g + 1) * RANK, :]) * step
        d = ORDER[g]
        if d == 0:
            whole[e] = value
            return
        code_tile(sums.at[e, d - 1], value)
        stage_two[e, d] = send(
            sums.at[e, d - 1],
            got_two.at[e, d - 1],
            two_send.at[e, d - 1],
            two_recv.at[e, d - 1],
            second_peer(e, shifted(second[e], d)),
        )

    def fan_out(e, b, k):
        for d in (2, 1, 3):
            tile = wire.at[e, first[e], b]
            copy = send(
                tile,
                tile,
                fan_send.at[e, k, d - 1],
                fan_recv.at[e, k, d - 1],
                first_peer(e, shifted(first[e], d)),
            )
            fans[e, k, d] = copy

    def sum_two(e):
        for d in (2, 1, 3):
            stage_two[e, d].wait_recv()
        value = whole[e]
        for k in range(SIDE - 1):
            value = value + number(got_two[e, k, :RANK, :]) * step_of(got_two[e, k, RANK:, :])
        value = jnp.transpose(value)
        whole[e] = value
        mine = second[e]
        tile = wire.at[e, first[e], mine]
        code_tile(tile, value)
        for d in (2, 1, 3):
            around[e, d] = send(
                tile,
                tile,
                ag_send.at[e, d - 1],
                ag_recv.at[e, d - 1],
                second_peer(e, shifted(mine, d)),
            )
        fan_out(e, mine, 0)

    def forward(e):
        for d in (1, 3, 2):
            around[e, d].wait_recv()
            fan_out(e, shifted(second[e], SIDE - d), d)

    stage_one = {}
    stage_two = {}
    around = {}
    fans = {}

    first_half(0)
    for d in (2, 1, 3):
        cross_of(0, d)
    pl.semaphore_wait(barrier, 2 * (SIDE - 1) + 3)
    send_one(0)
    first_half(1)
    gram_one[y] = gram[y]
    copies = to_column(lambda i: gram.at[i], gram_one.at[y], gram_send.at[0], gram_recv.at[0])
    for d in (2, 1, 3):
        cross_of(1, d)
    send_one(1)
    cross_of(0, 0)
    cross_of(1, 0)

    sum_one(0, 0)
    for copy in copies:
        copy.wait_recv()
    gram_two[x] = total_of(lambda i: gram_one[i])
    copies = to_row(gram_two.at[x], gram_send.at[1], gram_recv.at[1])
    sum_one(0, 1)
    sum_one(0, 2)
    sum_one(0, 3)
    sum_one(1, 0)
    for copy in copies:
        copy.wait_recv()
    gram_all[y] = total_of(lambda i: gram_two[i])
    copies = to_column(
        lambda i: gram_all.at[y], gram_all.at[y], gram_send.at[2], gram_recv.at[2]
    )
    sum_one(1, 1)
    sum_one(1, 2)
    sum_one(1, 3)
    sum_two(0)
    for copy in copies:
        copy.wait_recv()

    eye = (
        lax.broadcasted_iota(jnp.int32, (RANK, RANK), 0)
        == lax.broadcasted_iota(jnp.int32, (RANK, RANK), 1)
    ).astype(F32)
    for e in range(EXPERTS_HERE):
        for q in range(SIDE):
            work[e, q * QUARTER : (q + 1) * QUARTER, :RANK] = gram_all[q, e]
        work[e, :, RANK:] = eye
    for step in range(RANK // BLOCK):
        factor_block(work, step)
        if step == 1:
            sum_two(1)
        if step == 4:
            forward(0)
        if step == 12:
            forward(1)

    stacks = [stacked(work[e, :, RANK:]) for e in range(EXPERTS_HERE)]

    owners = (1, 4)
    for e in range(EXPERTS_HERE):
        value = times(raw[e], stacks[e])
        left[e] = value.astype(BF16)
        left_send[e] = (value * math.sqrt(D)).astype(BF16)
        last.append(
            send(
                left_send.at[e],
                left_got.at[e],
                own_send.at[e, 0],
                own_recv.at[e, 0],
                at_expert(owners[e]),
            )
        )

    order = [(k, d) for k in (0, 1, 3, 2) for d in (0, 1, 3, 2)]
    for e in range(EXPERTS_HERE):
        for pair in range(0, PEERS, 2):
            values = []
            places = []
            for k, d in order[pair : pair + 2]:
                if d:
                    fans[e, k, d].wait_recv()
                a = shifted(first[e], SIDE - d) if d else first[e]
                b = shifted(second[e], SIDE - k) if k else second[e]
                places.append(columns_of(e, a, b))
                values.append(
                    number(wire[e, a, b, :RANK, :]) * step_of(wire[e, a, b, RANK:, :])
                )
            right = times(jnp.concatenate(values, axis=0), stacks[e])
            for i, place_of in enumerate(places):
                tile = right[i * RANK : (i + 1) * RANK]
                span = pl.ds(pl.multiple_of(place_of * RANK, RANK), RANK)
                new_right[e, span, :] = tile
                squares[e, pl.ds(place_of, 1), :] = jnp.sum(tile * tile, axis=0, keepdims=True)

    scales = []
    for e in range(EXPERTS_HERE):
        mean = jnp.sum(squares[e], axis=0, keepdims=True) * (1.0 / FF)
        scales.append(lax.rsqrt(mean + EPSILON))
        right_send[e] = (times(whole[e], stacks[e]) * scales[e]).astype(BF16)
        last.append(
            send(
                right_send.at[e],
                right_got.at[e],
                own_send.at[e, 1],
                own_recv.at[e, 1],
                at_expert(owners[e]),
            )
        )

    for e in range(EXPERTS_HERE):
        for s in range(0, FF, 2 * RANK):
            span = slice(s, s + 2 * RANK)
            right = new_right[e, span, :]
            part = dot_last(left[e], (right * FEEDBACK).astype(BF16))
            buffer[e, :, span] = buffer[e, :, span] - part
            new_right[e, span, :] = right * scales[e]

    for copy in last:
        copy.wait_recv()
    for copy in sends:
        copy.wait_send()


def exchange(gradient, momentum, right_factor):
    dma = pltpu.SemaphoreType.DMA
    vmem = pltpu.VMEM
    n = EXPERTS_HERE
    tile = (RANK, RANK)
    others = SIDE - 1
    return pl.pallas_call(
        exchange_kernel,
        out_shape=(
            vmem((n, ROWS, FF), F32),
            vmem((n, FF, RANK), F32),
            vmem((n, ROWS, RANK), BF16),
            vmem((n, *tile), BF16),
        ),
        in_specs=[pl.BlockSpec(memory_space=pl.ANY)] * 3,
        out_specs=[pl.BlockSpec(memory_space=pltpu.VMEM)] * 4,
        scratch_shapes=[
            vmem((n, ROWS, FF), BF16),
            vmem((n, ROWS, FF), F32),
            vmem((n, FF, RANK), F32),
            vmem((n, PEERS, ROWS, RANK), BF16),
            vmem((n, PEERS, ROWS, RANK), BF16),
            vmem((n, ROWS, RANK), F32),
            vmem((n, 2 * RANK, ROWS), BF16),
            vmem((n, others, CHUNK, RANK), CODE),
            vmem((n, SIDE, *tile), F32),
            vmem((n, others, CHUNK, RANK), CODE),
            vmem((n, others, TILE, RANK), CODE),
            vmem((n, others, TILE, RANK), CODE),
            vmem((n, *tile), F32),
            vmem((n, SIDE, SIDE, TILE, RANK), CODE),
            vmem((SIDE, n, QUARTER, RANK), F32),
            vmem((SIDE, n, QUARTER, RANK), F32),
            vmem((SIDE, n, QUARTER, RANK), F32),
            vmem((SIDE, n, QUARTER, RANK), F32),
            vmem((n, RANK, 2 * RANK), F32),
            vmem((n, PEERS, RANK), F32),
            vmem((n, ROWS, RANK), BF16),
            vmem((n, ROWS, RANK), BF16),
            vmem((n, *tile), BF16),
            dma((n, 2 * PARTS + 1)),
            dma((n, SIDE, others)),
            dma((n, SIDE, others)),
            dma((n, others)),
            dma((n, others)),
            dma((3, others)),
            dma((3, others)),
            dma((n, others)),
            dma((n, others)),
            dma((n, SIDE, others)),
            dma((n, SIDE, others)),
            dma((n, 2)),
            dma((n, 2)),
        ],
        compiler_params=pltpu.CompilerParams(
            collective_id=0, has_side_effects=True, vmem_limit_bytes=44 * 2**20
        ),
        cost_estimate=pl.CostEstimate(
            flops=3 * 10**9, bytes_accessed=14 * 10**6, transcendentals=0
        ),
        name="exchange",
    )(gradient, momentum, right_factor)


STORES = 4
STORE_ROWS = ROWS // STORES


def store_kernel(place_ref, new_m, new_r, lgot, rgot, m_out, r_out, left_out, right_out, sem):
    group = lax.axis_index("expert")
    source = EXPERTS_HERE * lax.rem(group + GROUPS - 1, GROUPS)
    straight = place_ref[source] == EXPERTS_HERE * group
    copies = []
    for e in range(EXPERTS_HERE):
        for p in range(STORES):
            rows = pl.ds(p * STORE_ROWS, STORE_ROWS)
            copies.append((new_m.at[e, rows], m_out.at[e, rows]))
        copies.append((new_r.at[e], r_out.at[e]))
    for e in range(EXPERTS_HERE):
        pick = jnp.where(straight, e, 1 - e)
        copies.append((lgot.at[pick], left_out.at[e]))
        copies.append((rgot.at[pick], right_out.at[e]))
    started = []
    for k, (a, b) in enumerate(copies):
        copy = pltpu.make_async_copy(a, b, sem.at[k])
        copy.start()
        started.append(copy)
    for copy in started:
        copy.wait()


def store(placement, pieces):
    n = EXPERTS_HERE
    return pl.pallas_call(
        store_kernel,
        out_shape=(
            jax.ShapeDtypeStruct((n, ROWS, FF), F32),
            jax.ShapeDtypeStruct((n, FF, RANK), F32),
            jax.ShapeDtypeStruct((n, ROWS, RANK), BF16),
            jax.ShapeDtypeStruct((n, RANK, RANK), BF16),
        ),
        in_specs=[pl.BlockSpec(memory_space=pltpu.SMEM)]
        + [pl.BlockSpec(memory_space=pltpu.VMEM)] * 4,
        out_specs=[pl.BlockSpec(memory_space=pl.ANY)] * 4,
        scratch_shapes=[pltpu.SemaphoreType.DMA((n * (STORES + 3),))],
        compiler_params=pltpu.CompilerParams(vmem_limit_bytes=16 * 2**20),
        cost_estimate=pl.CostEstimate(flops=0, bytes_accessed=10 * 10**6, transcendentals=0),
        name="store",
    )(placement, *pieces)


def shards(gradient, momentum, right_factor, placement):
    pieces = exchange(gradient, momentum, right_factor)
    return store(placement, pieces)


def solution(mesh):
    placed = (P("expert", "fsdp", None), P("expert", "fsdp", None), P("expert", None, None), P())
    return jax.shard_map(
        shards,
        mesh=mesh,
        in_specs=placed,
        out_specs=(
            P("expert", "fsdp", None),
            P("expert", None, None),
            P("expert", "fsdp", None),
            P("expert", "fsdp", None),
        ),
        check_vma=False,
    )
```

```python
import functools
import math

import jax
import jax.numpy as jnp
from jax import lax
from jax.experimental import pallas as pl
from jax.experimental.pallas import tpu as pltpu
from jax.sharding import PartitionSpec as P

D = 7168
FEEDBACK = 0.05
EPSILON = 1e-06

EXPERTS_HERE = 2
ROWS = 448
FF = 2048
RANK = 128
SIDE = 4
PEERS = SIDE * SIDE
GROUPS = 8
PARTS = 2
PART_ROWS = ROWS // PARTS
BLOCK = 16
HEAD = 16
TILE = RANK + HEAD
CHUNK = SIDE * RANK + HEAD
ORDER = (2, 1, 3, 0)
QUARTER = RANK // SIDE
MESH = pl.DeviceIdType.MESH
F32 = jnp.float32
BF16 = jnp.bfloat16
CODE = jnp.int16


def split(value):
    high = value.astype(BF16)
    return high, (value - high.astype(F32)).astype(BF16)


def dot(a, b):
    return jnp.dot(a, b, preferred_element_type=F32)


def dot_last(a, b):
    return lax.dot_general(a, b, (((1,), (1,)), ((), ())), preferred_element_type=F32)


def dot_over_rows(a, b):
    return lax.dot_general(a, b, (((0,), (0,)), ((), ())), preferred_element_type=F32)


def factor_block(work, step):
    base = step * BLOCK
    line = lax.broadcasted_iota(jnp.int32, (BLOCK, 1), 0)
    for e in range(EXPERTS_HERE):
        rows = work[e, base : base + BLOCK, :]
        columns = [
            jnp.broadcast_to(rows[:, base + j : base + j + 1], (BLOCK, RANK)) for j in range(BLOCK)
        ]
        for j in range(BLOCK):
            inverse = lax.rsqrt(columns[j][j : j + 1, :])
            scaled = columns[j] * inverse
            below = jnp.where(line > j, scaled, 0.0)
            pivot_row = rows[j : j + 1, :] * jnp.concatenate([inverse, inverse], axis=1)
            below_wide = jnp.concatenate([below, below], axis=1)
            rows = jnp.where(line == j, pivot_row, rows - below_wide * pivot_row)
            for k in range(j + 1, BLOCK):
                columns[k] = columns[k] - below * scaled[k : k + 1, :]
        work[e, base : base + BLOCK, :] = rows
        done = base + BLOCK
        if done < RANK:
            upper = rows[:, :RANK]
            h = upper.astype(BF16).astype(F32)
            m = (upper - h).astype(BF16).astype(F32)
            l = upper - h - m
            hw = rows.astype(BF16).astype(F32)
            mw = (rows - hw).astype(BF16).astype(F32)
            lw = rows - hw - mw
            one = jnp.concatenate([h, h, m, h, m, l], axis=0).astype(BF16)
            two = jnp.concatenate([hw, mw, hw, lw, mw, hw], axis=0).astype(BF16)
            change = dot_over_rows(one, two)
            work[e, done:, :] = work[e, done:, :] - change[done:, :]


def stacked(inverse):
    high, low = split(jnp.transpose(inverse))
    wide = jnp.concatenate([high, low], axis=1)
    return jnp.concatenate([wide, wide], axis=0)


def times(value, stack):
    high, low = split(value)
    both = dot(jnp.concatenate([high, low], axis=1), stack)
    return both[:, :RANK] + both[:, RANK:]


def exponent_of(peak):
    peak = jnp.broadcast_to(jnp.maximum(peak, 1e-30), (HEAD, RANK))
    return jnp.ceil(jnp.log2(peak))


def coded(value, exponent):
    scaled = jnp.round(value * jnp.exp2(15.0 - exponent[:1]))
    return jnp.clip(scaled, -32767.0, 32767.0).astype(jnp.int32).astype(CODE)


def code_tile(target, value):
    exponent = exponent_of(jnp.max(jnp.abs(value), axis=0, keepdims=True))
    target[:RANK, :] = coded(value, exponent)
    target[RANK:, :] = exponent.astype(jnp.int32).astype(CODE)


def step_of(head):
    return jnp.exp2(head.astype(jnp.int32).astype(F32)[:1] - 15.0)


def number(code):
    return code.astype(jnp.int32).astype(F32)


def exchange_kernel(
    grad_hbm,
    moment_hbm,
    factor_hbm,
    buffer,
    new_right,
    left_got,
    right_got,
    grad,
    moment,
    factor,
    high_part,
    low_part,
    raw,
    turned,
    cross,
    own_one,
    got_one,
    sums,
    got_two,
    whole,
    wire,
    gram,
    gram_one,
    gram_two,
    gram_all,
    work,
    squares,
    left,
    left_send,
    right_send,
    load_sem,
    one_send,
    one_recv,
    two_send,
    two_recv,
    gram_send,
    gram_recv,
    ag_send,
    ag_recv,
    fan_send,
    fan_recv,
    own_send,
    own_recv,
):
    place = lax.axis_index("fsdp")
    group = lax.axis_index("expert")
    x = lax.rem(place, SIDE)
    y = lax.div(place, SIDE)

    def along_x(index):
        return {"fsdp": y * SIDE + index, "expert": group}

    def along_y(index):
        return {"fsdp": index * SIDE + x, "expert": group}

    def at_expert(shift):
        return {"fsdp": place, "expert": lax.rem(group + shift, GROUPS)}

    def shifted(v, d):
        return lax.rem(v + d, SIDE)

    first = (x, y)
    second = (y, x)

    def first_peer(e, index):
        return along_x(index) if e == 0 else along_y(index)

    def second_peer(e, index):
        return along_y(index) if e == 0 else along_x(index)

    def columns_of(e, a, b):
        return b * SIDE + a if e == 0 else a * SIDE + b

    barrier = pltpu.get_barrier_semaphore()
    for d in range(1, SIDE):
        for peer in (along_x(shifted(x, d)), along_y(shifted(y, d))):
            pl.semaphore_signal(barrier, inc=1, device_id=peer, device_id_type=MESH)
    for d in (1, 4, GROUPS - 1):
        pl.semaphore_signal(barrier, inc=1, device_id=at_expert(d), device_id_type=MESH)

    loads = {}

    def load(e, p):
        if p == PARTS:
            pieces = ((factor_hbm.at[1 - e], factor.at[e]),)
        else:
            rows = pl.ds(p * PART_ROWS, PART_ROWS)
            pieces = (
                (grad_hbm.at[1 - e, rows], grad.at[e, rows]),
                (moment_hbm.at[1 - e, rows], moment.at[e, rows]),
            )
        for k, (source, target) in enumerate(pieces):
            copy = pltpu.make_async_copy(source, target, load_sem.at[e, 2 * p + k])
            copy.start()
            loads[e, 2 * p + k] = copy

    load(0, PARTS)
    for p in range(PARTS):
        load(0, p)

    sends = []
    last = []

    def send(source, target, send_sem, recv_sem, peer):
        copy = pltpu.make_async_remote_copy(
            src_ref=source,
            dst_ref=target,
            send_sem=send_sem,
            recv_sem=recv_sem,
            device_id=peer,
            device_id_type=MESH,
        )
        copy.start()
        sends.append(copy)
        return copy

    def total_of(slots):
        return (slots(0) + slots(1)) + (slots(2) + slots(3))

    def to_column(source, target, send_sems, recv_sems):
        return [
            send(
                source(shifted(y, d)),
                target,
                send_sems.at[d - 1],
                recv_sems.at[d - 1],
                along_y(shifted(y, d)),
            )
            for d in (2, 1, 3)
        ]

    def to_row(slot, send_sems, recv_sems):
        return [
            send(slot, slot, send_sems.at[d - 1], recv_sems.at[d - 1], along_x(shifted(x, d)))
            for d in (2, 1, 3)
        ]

    def first_half(e):
        loads[e, 2 * PARTS].wait()
        if e == 0:
            load(1, PARTS)
        value = factor[e]
        norm = jnp.sum(value * value, axis=0, keepdims=True)
        high, low = split(value * lax.rsqrt(jnp.maximum(norm, 1e-30)))
        weights = jnp.concatenate([high, low], axis=1)
        for p in range(PARTS):
            loads[e, 2 * p].wait()
            loads[e, 2 * p + 1].wait()
            if e == 0:
                load(1, p)
            rows = slice(p * PART_ROWS, (p + 1) * PART_ROWS)
            total = moment[e, rows, :] + grad[e, rows, :].astype(F32)
            buffer[e, rows, :] = total
            bh, bl = split(total)
            for s in range(PEERS):
                high_part[e, s, rows, :] = bh[:, s * RANK : (s + 1) * RANK]
                low_part[e, s, rows, :] = bl[:, s * RANK : (s + 1) * RANK]
            product = dot(bh, weights)
            raw[e, rows, :] = product[:, :RANK] + (product[:, RANK:] + dot(bl, high))
        lh, ll = split(raw[e])
        th, tl = split(jnp.transpose(raw[e]))
        turned[e] = jnp.concatenate([th, tl], axis=0)
        four = dot(turned[e], jnp.concatenate([lh, ll], axis=1))
        value = four[:RANK, :RANK] + four[:RANK, RANK:] + (four[RANK:, :RANK] + four[RANK:, RANK:])
        for q in range(SIDE):
            gram[q, e] = value[q * QUARTER : (q + 1) * QUARTER, :]

    def cross_of(e, d):
        a = shifted(first[e], d)
        pairs = []
        for k0, k1 in ((ORDER[0], ORDER[1]), (ORDER[2], ORDER[3])):
            s0 = columns_of(e, a, shifted(second[e], k0))
            s1 = columns_of(e, a, shifted(second[e], k1))
            bh = jnp.concatenate([high_part[e, s0], high_part[e, s1]], axis=1)
            bl = jnp.concatenate([low_part[e, s0], low_part[e, s1]], axis=1)
            value = dot(turned[e], bh)
            pairs.append(value[:RANK] + (value[RANK:] + dot(turned[e, :RANK, :], bl)))
        tiles = [pairs[g // 2][:, (g % 2) * RANK : (g % 2 + 1) * RANK] for g in range(SIDE)]
        if d == 0:
            for g in range(SIDE):
                own_one[e, g] = tiles[g]
            return
        peak = jnp.maximum(*[jnp.max(jnp.abs(value), axis=0, keepdims=True) for value in pairs])
        exponent = exponent_of(jnp.maximum(peak[:, :RANK], peak[:, RANK:]))
        cross[e, d - 1, :HEAD, :] = exponent.astype(jnp.int32).astype(CODE)
        for g in range(SIDE):
            cross[e, d - 1, HEAD + g * RANK : HEAD + (g + 1) * RANK, :] = coded(tiles[g], exponent)

    def send_one(e):
        for g in range(SIDE):
            start, end = (HEAD + g * RANK if g else 0), HEAD + (g + 1) * RANK
            for d in (2, 1, 3):
                stage_one[e, g, d] = send(
                    cross.at[e, d - 1, start:end],
                    got_one.at[e, d - 1, start:end],
                    one_send.at[e, g, d - 1],
                    one_recv.at[e, g, d - 1],
                    first_peer(e, shifted(first[e], d)),
                )

    def sum_one(e, g):
        for d in (2, 1, 3):
            stage_one[e, g, d].wait_recv()
        value = own_one[e, g]
        for k in range(SIDE - 1):
            step = step_of(got_one[e, k, :HEAD, :])
            value = value + number(got_one[e, k, HEAD + g * RANK : HEAD + (g + 1) * RANK, :]) * step
        d = ORDER[g]
        if d == 0:
            whole[e] = value
            return
        code_tile(sums.at[e, d - 1], value)
        stage_two[e, d] = send(
            sums.at[e, d - 1],
            got_two.at[e, d - 1],
            two_send.at[e, d - 1],
            two_recv.at[e, d - 1],
            second_peer(e, shifted(second[e], d)),
        )

    def fan_out(e, b, k):
        for d in (2, 1, 3):
            tile = wire.at[e, first[e], b]
            copy = send(
                tile,
                tile,
                fan_send.at[e, k, d - 1],
                fan_recv.at[e, k, d - 1],
                first_peer(e, shifted(first[e], d)),
            )
            fans[e, k, d] = copy

    def sum_two(e):
        for d in (2, 1, 3):
            stage_two[e, d].wait_recv()
        value = whole[e]
        for k in range(SIDE - 1):
            value = value + number(got_two[e, k, :RANK, :]) * step_of(got_two[e, k, RANK:, :])
        value = jnp.transpose(value)
        whole[e] = value
        mine = second[e]
        tile = wire.at[e, first[e], mine]
        code_tile(tile, value)
        for d in (2, 1, 3):
            around[e, d] = send(
                tile,
                tile,
                ag_send.at[e, d - 1],
                ag_recv.at[e, d - 1],
                second_peer(e, shifted(mine, d)),
            )
        fan_out(e, mine, 0)

    def forward(e):
        for d in (1, 3, 2):
            around[e, d].wait_recv()
            fan_out(e, shifted(second[e], SIDE - d), d)

    stage_one = {}
    stage_two = {}
    around = {}
    fans = {}

    first_half(0)
    for d in (2, 1, 3):
        cross_of(0, d)
    pl.semaphore_wait(barrier, 2 * (SIDE - 1) + 3)
    send_one(0)
    first_half(1)
    gram_one[y] = gram[y]
    copies = to_column(lambda i: gram.at[i], gram_one.at[y], gram_send.at[0], gram_recv.at[0])
    for d in (2, 1, 3):
        cross_of(1, d)
    send_one(1)
    cross_of(0, 0)
    cross_of(1, 0)

    def gram_next(stage, copies):
        for copy in copies:
            copy.wait_recv()
        if stage == 1:
            gram_two[x] = total_of(lambda i: gram_one[i])
            return to_row(gram_two.at[x], gram_send.at[1], gram_recv.at[1])
        if stage == 2:
            gram_all[y] = total_of(lambda i: gram_two[i])
            return to_column(
                lambda i: gram_all.at[y], gram_all.at[y], gram_send.at[2], gram_recv.at[2]
            )
        return None

    sum_one(0, 0)
    copies = gram_next(1, copies)
    sum_one(0, 1)
    sum_one(0, 2)
    sum_one(0, 3)
    sum_one(1, 0)
    copies = gram_next(2, copies)
    sum_one(1, 1)
    sum_one(1, 2)
    sum_one(1, 3)
    sum_two(0)
    sum_two(1)
    copies = gram_next(3, copies)

    eye = (
        lax.broadcasted_iota(jnp.int32, (RANK, RANK), 0)
        == lax.broadcasted_iota(jnp.int32, (RANK, RANK), 1)
    ).astype(F32)
    for e in range(EXPERTS_HERE):
        for q in range(SIDE):
            work[e, q * QUARTER : (q + 1) * QUARTER, :RANK] = gram_all[q, e]
        work[e, :, RANK:] = eye
    for step in range(RANK // BLOCK):
        factor_block(work, step)
        if step == 1:
            forward(0)
        if step == 5:
            forward(1)

    stacks = [stacked(work[e, :, RANK:]) for e in range(EXPERTS_HERE)]

    owners = (4, 1)
    for e in range(EXPERTS_HERE):
        value = times(raw[e], stacks[e])
        left[e] = value.astype(BF16)
        left_send[e] = (value * math.sqrt(D)).astype(BF16)
        last.append(
            send(
                left_send.at[e],
                left_got.at[e],
                own_send.at[e, 0],
                own_recv.at[e, 0],
                at_expert(owners[e]),
            )
        )

    order = [(k, d) for k in (0, 1, 3, 2) for d in (0, 1, 3, 2)]
    scales = {}
    for e in range(EXPERTS_HERE):
        for pair in range(0, PEERS, 2):
            values = []
            places = []
            for k, d in order[pair : pair + 2]:
                if d:
                    fans[e, k, d].wait_recv()
                a = shifted(first[e], SIDE - d) if d else first[e]
                b = shifted(second[e], SIDE - k) if k else second[e]
                places.append(columns_of(e, a, b))
                values.append(
                    number(wire[e, a, b, :RANK, :]) * step_of(wire[e, a, b, RANK:, :])
                )
            right = times(jnp.concatenate(values, axis=0), stacks[e])
            for i, place_of in enumerate(places):
                tile = right[i * RANK : (i + 1) * RANK]
                span = pl.ds(pl.multiple_of(place_of * RANK, RANK), RANK)
                new_right[e, span, :] = tile
                squares[e, pl.ds(place_of, 1), :] = jnp.sum(tile * tile, axis=0, keepdims=True)

        mean = jnp.sum(squares[e], axis=0, keepdims=True) * (1.0 / FF)
        scales[e] = lax.rsqrt(mean + EPSILON)
        right_send[e] = (times(whole[e], stacks[e]) * scales[e]).astype(BF16)
        last.append(
            send(
                right_send.at[e],
                right_got.at[e],
                own_send.at[e, 1],
                own_recv.at[e, 1],
                at_expert(owners[e]),
            )
        )

    for e in range(EXPERTS_HERE):
        for s in range(0, FF, 2 * RANK):
            span = slice(s, s + 2 * RANK)
            right = new_right[e, span, :]
            part = dot_last(left[e], (right * FEEDBACK).astype(BF16))
            buffer[e, :, span] = buffer[e, :, span] - part
            new_right[e, span, :] = right * scales[e]

    for copy in sends:
        copy.wait_send()
    for copy in last:
        copy.wait_recv()


def exchange(gradient, momentum, right_factor):
    dma = pltpu.SemaphoreType.DMA
    vmem = pltpu.VMEM
    n = EXPERTS_HERE
    tile = (RANK, RANK)
    others = SIDE - 1
    return pl.pallas_call(
        exchange_kernel,
        out_shape=(
            vmem((n, ROWS, FF), F32),
            vmem((n, FF, RANK), F32),
            vmem((n, ROWS, RANK), BF16),
            vmem((n, *tile), BF16),
        ),
        in_specs=[pl.BlockSpec(memory_space=pl.ANY)] * 3,
        out_specs=[pl.BlockSpec(memory_space=pltpu.VMEM)] * 4,
        scratch_shapes=[
            vmem((n, ROWS, FF), BF16),
            vmem((n, ROWS, FF), F32),
            vmem((n, FF, RANK), F32),
            vmem((n, PEERS, ROWS, RANK), BF16),
            vmem((n, PEERS, ROWS, RANK), BF16),
            vmem((n, ROWS, RANK), F32),
            vmem((n, 2 * RANK, ROWS), BF16),
            vmem((n, others, CHUNK, RANK), CODE),
            vmem((n, SIDE, *tile), F32),
            vmem((n, others, CHUNK, RANK), CODE),
            vmem((n, others, TILE, RANK), CODE),
            vmem((n, others, TILE, RANK), CODE),
            vmem((n, *tile), F32),
            vmem((n, SIDE, SIDE, TILE, RANK), CODE),
            vmem((SIDE, n, QUARTER, RANK), F32),
            vmem((SIDE, n, QUARTER, RANK), F32),
            vmem((SIDE, n, QUARTER, RANK), F32),
            vmem((SIDE, n, QUARTER, RANK), F32),
            vmem((n, RANK, 2 * RANK), F32),
            vmem((n, PEERS, RANK), F32),
            vmem((n, ROWS, RANK), BF16),
            vmem((n, ROWS, RANK), BF16),
            vmem((n, *tile), BF16),
            dma((n, 2 * PARTS + 1)),
            dma((n, SIDE, others)),
            dma((n, SIDE, others)),
            dma((n, others)),
            dma((n, others)),
            dma((3, others)),
            dma((3, others)),
            dma((n, others)),
            dma((n, others)),
            dma((n, SIDE, others)),
            dma((n, SIDE, others)),
            dma((n, 2)),
            dma((n, 2)),
        ],
        compiler_params=pltpu.CompilerParams(
            collective_id=0, has_side_effects=True, vmem_limit_bytes=44 * 2**20
        ),
        cost_estimate=pl.CostEstimate(
            flops=3 * 10**9, bytes_accessed=14 * 10**6, transcendentals=0
        ),
        name="exchange",
    )(gradient, momentum, right_factor)


STORES = 4
STORE_ROWS = ROWS // STORES


def store_kernel(place_ref, new_m, new_r, lgot, rgot, m_out, r_out, left_out, right_out, sem):
    group = lax.axis_index("expert")
    source = EXPERTS_HERE * lax.rem(group + GROUPS - 1, GROUPS)
    straight = place_ref[source] == EXPERTS_HERE * group
    copies = []
    for e in range(EXPERTS_HERE):
        for p in range(STORES):
            rows = pl.ds(p * STORE_ROWS, STORE_ROWS)
            copies.append((new_m.at[1 - e, rows], m_out.at[e, rows]))
        copies.append((new_r.at[1 - e], r_out.at[e]))
    for e in range(EXPERTS_HERE):
        pick = jnp.where(straight, 1 - e, e)
        copies.append((lgot.at[pick], left_out.at[e]))
        copies.append((rgot.at[pick], right_out.at[e]))
    started = []
    for k, (a, b) in enumerate(copies):
        copy = pltpu.make_async_copy(a, b, sem.at[k])
        copy.start()
        started.append(copy)
    for copy in started:
        copy.wait()


def store(placement, pieces):
    n = EXPERTS_HERE
    return pl.pallas_call(
        store_kernel,
        out_shape=(
            jax.ShapeDtypeStruct((n, ROWS, FF), F32),
            jax.ShapeDtypeStruct((n, FF, RANK), F32),
            jax.ShapeDtypeStruct((n, ROWS, RANK), BF16),
            jax.ShapeDtypeStruct((n, RANK, RANK), BF16),
        ),
        in_specs=[pl.BlockSpec(memory_space=pltpu.SMEM)]
        + [pl.BlockSpec(memory_space=pltpu.VMEM)] * 4,
        out_specs=[pl.BlockSpec(memory_space=pl.ANY)] * 4,
        scratch_shapes=[pltpu.SemaphoreType.DMA((n * (STORES + 3),))],
        compiler_params=pltpu.CompilerParams(vmem_limit_bytes=16 * 2**20),
        cost_estimate=pl.CostEstimate(flops=0, bytes_accessed=10 * 10**6, transcendentals=0),
        name="store",
    )(placement, *pieces)


def shards(gradient, momentum, right_factor, placement):
    pieces = exchange(gradient, momentum, right_factor)
    return store(placement, pieces)


def solution(mesh):
    placed = (P("expert", "fsdp", None), P("expert", "fsdp", None), P("expert", None, None), P())
    return jax.shard_map(
        shards,
        mesh=mesh,
        in_specs=placed,
        out_specs=(
            P("expert", "fsdp", None),
            P("expert", None, None),
            P("expert", "fsdp", None),
            P("expert", "fsdp", None),
        ),
        check_vma=False,
    )
```
